32 devices in a mesh: lon: 16 (over z, y, core), lat: 2 (over x).
Axes of the slice: x: 2, y: 2, z: 4, core: 2. Of those that a mesh axis runs over, the one named last changes fastest.
Arguments:
- field: float32 [2, 12, 1280, 640], P(None, 'lat', 'lon'), may hold values from -6 to 6
- spectral_filter: float32 [2, 7, 640, 640], P(None, None, None, 'lon'), may hold values from -2 to 2
- w_in: bfloat16 [640, 1280], replicated, may hold values from -0.25 to 0.25
- w_out: bfloat16 [1280, 640], replicated, may hold values from -0.15625 to 0.15625
Outputs:
- result: float32 [2, 12, 1280, 640], P(None, 'lat', 'lon')
The draws below stay inside these ranges and needn't reach their ends.
All inputs are finite; a program needn't handle non-finite values.
Results may differ from the reference program's by a relative error of at most 0.0016.
Values sent between devices are 32-bit elements; how exact they have to be, the bound alone decides.
A program may use at most 64 MiB of HBM per device.

```python
import jax
import jax.numpy as jnp
from jax import lax

C = 640
HID = 1280
LON = 1280
ENS = 2
TAPS = 7
MODES = 640
NLAT = 12


def shard_levels(key, dims, shards, smallest, largest):
    def one(axis_at, parts):
        heights = jax.random.uniform(jax.random.fold_in(jax.random.fold_in(key, 6), axis_at), (parts,), jnp.float32, smallest / len(shards), largest / len(shards))
        return jnp.repeat(jnp.exp(heights), dims[axis_at] // parts).reshape((-1,) + (1,) * (len(dims) - axis_at - 1))

    factor_of = one(*shards[0])
    for cut in shards[1:]:
        factor_of = factor_of * one(*cut)
    return factor_of


def scatter_about(own_key, extent, scale, most, split=(), held_as=jnp.bfloat16):
    array = jax.random.normal(own_key, extent, jnp.float32) * scale
    if len(split) > 0:
        array = shard_levels(own_key, extent, split, -0.22, 0.18) * array
    return jnp.clip(array, min=-most, max=most).astype(held_as)


def setup_inputs(seed: int = 0) -> dict:
    seeds = jax.random.split(jax.random.key(seed), 5)
    return {
        "field": scatter_about(seeds[0], (ENS, NLAT, LON, C), 1.0, 6.0, ((1, 2), (2, 16)), jnp.float32),
        "spectral_filter": scatter_about(seeds[1], (2, TAPS, MODES, C), 0.3, 2.0, ((3, 16),), jnp.float32),
        "w_in": scatter_about(seeds[2], (C, HID), C ** -0.5, 0.25),
        "w_out": scatter_about(seeds[3], (HID, C), HID ** -0.5, 0.15625),
    }


def member_block(field_one, filter_complex, w_in, w_out):
    spectrum = jnp.fft.rfft(field_one, axis=1)[:, :MODES, :]
    padded = jnp.pad(spectrum, ((3, 3), (0, 0), (0, 0)))
    convolved = filter_complex[0][None] * padded[0:NLAT]
    for offset in range(1, TAPS):
        convolved = convolved + filter_complex[offset][None] * padded[offset:offset + NLAT]
    full = jnp.pad(convolved, ((0, 0), (0, LON // 2 + 1 - MODES), (0, 0)))
    conv_grid = jnp.fft.irfft(full, n=LON, axis=1).astype(field_one.dtype)
    mixed = field_one + conv_grid
    rows = mixed.reshape(-1, C)
    center = lax.optimization_barrier(jnp.mean(rows, axis=1, keepdims=True))
    spread = lax.optimization_barrier(jnp.mean((rows - center) ** 2, axis=1, keepdims=True))
    normed = ((rows - center) / jnp.sqrt(spread + 1e-05)).astype(jnp.bfloat16)
    before = jnp.dot(normed, w_in, preferred_element_type=jnp.float32)
    hidden = jax.nn.gelu(before, approximate=False).astype(jnp.bfloat16)
    update = jnp.dot(hidden, w_out, preferred_element_type=jnp.float32)
    return mixed + update.reshape(mixed.shape).astype(mixed.dtype)

def reference(field, spectral_filter, w_in, w_out):
    filter_complex = spectral_filter[0] + 1j * spectral_filter[1]

    def one_member(field_one):
        return member_block(field_one, filter_complex, w_in, w_out)
    return lax.map(one_member, field)
```

```python
import functools

import jax
import jax.numpy as jnp
import ml_dtypes
import numpy as np
from jax import lax
from jax.experimental import pallas as pl
from jax.experimental.pallas import tpu as pltpu
from jax.sharding import PartitionSpec as P

LANES = 128
HALO = 3
TAPS = 7
MESH = pl.DeviceIdType.MESH
F32 = jnp.float32
BF16 = jnp.bfloat16


def split_table(table):
    high = table.astype(ml_dtypes.bfloat16)
    low = (table - high.astype(np.float64)).astype(ml_dtypes.bfloat16)
    return high, low


def tables(length):
    modes = length // 2
    orders = np.arange(modes, dtype=np.int64)[:, None]
    places = np.arange(length, dtype=np.int64)[None, :]
    angles = 2.0 * np.pi / length * (orders * places % length).astype(np.float64)
    forward = np.concatenate([np.cos(angles), -np.sin(angles)], axis=0)
    weights = np.where(np.arange(modes) == 0, 1.0, 2.0) / length
    inverse = (forward * np.concatenate([weights, weights])[:, None]).T
    return split_table(forward) + split_table(np.ascontiguousarray(inverse))


def lane_index(rows):
    return lax.broadcasted_iota(jnp.int32, (rows, LANES), 1)


def rolled(block, shift):
    shift = shift % LANES
    return block if shift == 0 else pltpu.roll(block, shift, 1)


def split_value(value):
    high = value.astype(BF16)
    return high, (value - high.astype(F32)).astype(BF16)


def dot3(a_high, a_low, b_high, b_low):
    total = jnp.dot(a_high, b_high, preferred_element_type=F32)
    total += jnp.dot(a_low, b_high, preferred_element_type=F32)
    return total + jnp.dot(a_high, b_low, preferred_element_type=F32)


def kernel(
    groups, lats, field_hbm, filter_hbm, fwd_high_hbm, fwd_low_hbm, inv_high_hbm, inv_low_hbm, w_in_hbm, w_out_hbm,
    out_hbm, field, filt, fwd_high, fwd_low, inv_high, inv_low, w_in, w_out,
    packed, grid, grid_high, grid_low, spec, stack, coef, spec_high, spec_low, conv, back, mixed, normed, hidden, result,
    load_sem, send_sem, recv_sem, halo_send, halo_recv, home_send, home_recv, out_sem,
):
    members, rows_lat, lon_local, channels = field.shape
    width = channels // groups
    length = lon_local * groups
    modes = length // 2
    per_member = rows_lat // HALO
    chunks = members * per_member
    me = lax.axis_index("lon")
    lat = lax.axis_index("lat")
    own = pl.ds(pl.multiple_of(me * lon_local, 8), lon_local)
    has_low = lat > 0
    has_high = lat < lats - 1

    loads = [
        pltpu.make_async_copy(src, dst, load_sem.at[n])
        for n, (src, dst) in enumerate(
            [
                (field_hbm, field),
                (filter_hbm, filt),
                (fwd_high_hbm, fwd_high),
                (fwd_low_hbm, fwd_low),
                (inv_high_hbm, inv_high),
                (inv_low_hbm, inv_low),
                (w_in_hbm, w_in),
                (w_out_hbm, w_out),
            ]
        )
    ]
    for load in loads:
        load.start()

    barrier = pltpu.get_barrier_semaphore()

    def greet(d, carry):
        pl.semaphore_signal(barrier, inc=1, device_id=(lax.rem(me + d, groups), lat), device_id_type=MESH)
        return carry

    lax.fori_loop(1, groups, greet, 0)

    @pl.when(has_low)
    def _():
        pl.semaphore_signal(barrier, inc=1, device_id=(me, lat - 1), device_id_type=MESH)

    @pl.when(has_high)
    def _():
        pl.semaphore_signal(barrier, inc=1, device_id=(me, lat + 1), device_id_type=MESH)

    def pack(chunk):
        member, part = chunk // per_member, chunk % per_member
        lanes = lane_index(lon_local)
        for g in range(groups):
            total = jnp.zeros((lon_local, LANES), F32)
            for j in range(HALO):
                start = g * width
                for b in range(start // LANES, (start + width - 1) // LANES + 1):
                    first = max(start, b * LANES) - start
                    last = min(start + width, (b + 1) * LANES) - start
                    block = field[member, part * HALO + j, :, b * LANES : (b + 1) * LANES]
                    moved = rolled(block, j * width - (start - b * LANES))
                    keep = (lanes >= j * width + first) & (lanes < j * width + last)
                    total = jnp.where(keep, moved, total)
            packed[chunk, g] = total
        grid[chunk, own, :] = packed[chunk, me]

    def outward(chunk, d):
        peer = lax.rem(me + d, groups)
        return pltpu.make_async_remote_copy(
            src_ref=packed.at[chunk, peer],
            dst_ref=grid.at[chunk, own],
            send_sem=send_sem.at[chunk, d],
            recv_sem=recv_sem.at[chunk, d],
            device_id=(peer, lat),
            device_id_type=MESH,
        )

    def homeward(chunk, d):
        peer = lax.rem(me + d, groups)
        return pltpu.make_async_remote_copy(
            src_ref=conv.at[chunk, pl.ds(pl.multiple_of(peer * lon_local, 8), lon_local)],
            dst_ref=back.at[chunk, me],
            send_sem=home_send.at[chunk, d],
            recv_sem=home_recv.at[chunk, d],
            device_id=(peer, lat),
            device_id_type=MESH,
        )

    def each(action):
        def step(d, carry):
            action(d)
            return carry

        lax.fori_loop(1, groups, step, 0)

    def halo_up(member):
        return pltpu.make_async_remote_copy(
            src_ref=spec.at[member, per_member],
            dst_ref=spec.at[member, 0],
            send_sem=halo_send.at[member, 0],
            recv_sem=halo_recv.at[member, 0],
            device_id=(me, lat + 1),
            device_id_type=MESH,
        )

    def halo_down(member):
        return pltpu.make_async_remote_copy(
            src_ref=spec.at[member, 1],
            dst_ref=spec.at[member, per_member + 1],
            send_sem=halo_send.at[member, 1],
            recv_sem=halo_recv.at[member, 1],
            device_id=(me, lat - 1),
            device_id_type=MESH,
        )

    loads[0].wait()
    pack(0)
    others = groups - 1 + has_low.astype(jnp.int32) + has_high.astype(jnp.int32)
    pl.semaphore_wait(barrier, others)
    each(lambda d: outward(0, d).start())

    def pack_and_send(chunk, carry):
        pack(chunk)
        each(lambda d: outward(chunk, d).start())
        return carry

    lax.fori_loop(1, chunks, pack_and_send, 0)

    @pl.when(jnp.logical_not(has_low))
    def _():
        for member in range(members):
            spec[member, 0] = jnp.zeros((length, LANES), F32)

    @pl.when(jnp.logical_not(has_high))
    def _():
        for member in range(members):
            spec[member, per_member + 1] = jnp.zeros((length, LANES), F32)

    stack[...] = jnp.zeros_like(stack)
    loads[1].wait()

    def spread(n, carry):
        part = filt[n // TAPS, n % TAPS]
        for j in range(HALO):
            stack[j * width : (j + 1) * width, :] = part
        coef[n // TAPS, n % TAPS] = stack[...].T
        return carry

    lax.fori_loop(0, 2 * TAPS, spread, 0)
    for load in loads[2:]:
        load.wait()

    tile = 256
    columns = per_member * LANES

    def transform(member):
        for part in range(per_member):
            chunk = member * per_member + part
            each(lambda d: outward(chunk, d).wait_recv())

            def halve(t, carry):
                rows = pl.ds(pl.multiple_of(t * tile, tile), tile)
                high, low = split_value(grid[chunk, rows, :])
                grid_high[rows, part * LANES : (part + 1) * LANES] = high
                grid_low[rows, part * LANES : (part + 1) * LANES] = low
                return carry

            lax.fori_loop(0, length // tile, halve, 0)

        def step(t, carry):
            rows = pl.ds(pl.multiple_of(t * tile, tile), tile)
            value = dot3(fwd_high[rows, :], fwd_low[rows, :], grid_high[...], grid_low[...])
            for part in range(per_member):
                spec[member, part + 1, rows, :] = value[:, part * LANES : (part + 1) * LANES]
            return carry

        lax.fori_loop(0, length // tile, step, 0)

        @pl.when(has_high)
        def _():
            halo_up(member).start()

        @pl.when(has_low)
        def _():
            halo_down(member).start()

    def filtered(member):
        @pl.when(has_low)
        def _():
            halo_up(member).wait_recv()

        @pl.when(has_high)
        def _():
            halo_down(member).wait_recv()

        step_rows = 16
        lanes = lane_index(step_rows)

        def step(t, carry):
            at = pl.multiple_of(t * step_rows, step_rows)
            real_rows = pl.ds(at, step_rows)
            imag_rows = pl.ds(modes + at, step_rows)
            real = [spec[member, p, real_rows, :] for p in range(per_member + 2)]
            imag = [spec[member, p, imag_rows, :] for p in range(per_member + 2)]

            def at_shift(values, p, s):
                if s % HALO == 0:
                    return values[p + s // HALO]
                if s > 0:
                    here, there, cut = values[p], values[p + 1], (HALO - s) * width
                    return jnp.where(lanes < cut, rolled(here, -s * width), rolled(there, cut))
                here, there, cut = values[p], values[p - 1], -s * width
                return jnp.where(lanes < cut, rolled(there, -(HALO + s) * width), rolled(here, cut))

            for part in range(per_member):
                total_real = jnp.zeros((step_rows, LANES), F32)
                total_imag = jnp.zeros((step_rows, LANES), F32)
                for d in range(TAPS):
                    h_real = coef[0, d, real_rows, :]
                    h_imag = coef[1, d, real_rows, :]
                    x_real = at_shift(real, part + 1, d - HALO)
                    x_imag = at_shift(imag, part + 1, d - HALO)
                    total_real += h_real * x_real - h_imag * x_imag
                    total_imag += h_real * x_imag + h_imag * x_real
                side = slice(part * LANES, (part + 1) * LANES)
                high, low = split_value(total_real)
                spec_high[real_rows, side] = high
                spec_low[real_rows, side] = low
                high, low = split_value(total_imag)
                spec_high[imag_rows, side] = high
                spec_low[imag_rows, side] = low
            return carry

        lax.fori_loop(0, modes // step_rows, step, 0)

    def inverse(member):
        def step(t, carry):
            rows = pl.ds(pl.multiple_of(t * tile, tile), tile)
            value = dot3(inv_high[rows, :], inv_low[rows, :], spec_high[...], spec_low[...])
            for part in range(per_member):
                conv[member * per_member + part, rows, :] = value[:, part * LANES : (part + 1) * LANES]
            return carry

        lax.fori_loop(0, length // tile, step, 0)
        for part in range(per_member):
            chunk = member * per_member + part
            each(lambda d: homeward(chunk, d).start())
            back[chunk, me] = conv[chunk, own, :]

    def finish(chunk):
        member, part = chunk // per_member, chunk % per_member
        each(lambda d: homeward(chunk, d).wait_recv())
        lanes = lane_index(lon_local)
        for j in range(HALO):
            for b in range(channels // LANES):
                total = jnp.zeros((lon_local, LANES), F32)
                for g in range(b * LANES // width, ((b + 1) * LANES - 1) // width + 1):
                    start = g * width - b * LANES
                    moved = rolled(back[chunk, g], start - j * width)
                    keep = (lanes >= start) & (lanes < start + width)
                    total = jnp.where(keep, moved, total)
                side = slice(b * LANES, (b + 1) * LANES)
                mixed[j * lon_local : (j + 1) * lon_local, side] = field[member, part * HALO + j, :, side] + total
        rows = mixed[...]
        center = jnp.mean(rows, axis=1, keepdims=True)
        away = rows - center
        variance = jnp.mean(away * away, axis=1, keepdims=True)
        normed[...] = (away / jnp.sqrt(variance + 1e-05)).astype(BF16)
        hidden_units = hidden.shape[1]
        for q in range(hidden_units // 256):
            side = slice(q * 256, (q + 1) * 256)
            before = jnp.dot(normed[...], w_in[:, side], preferred_element_type=F32)
            value = 0.5 * before * (1.0 + lax.erf(before * np.float32(np.sqrt(0.5))))
            hidden[:, side] = value.astype(BF16)
        for b in range(channels // LANES):
            side = slice(b * LANES, (b + 1) * LANES)
            update = jnp.dot(hidden[...], w_out[:, side], preferred_element_type=F32) + mixed[:, side]
            for j in range(HALO):
                result[member, part * HALO + j, :, side] = update[j * lon_local : (j + 1) * lon_local]
        saved(chunk).start()

    def saved(chunk):
        member, part = chunk // per_member, chunk % per_member
        place = pl.ds(part * HALO, HALO)
        return pltpu.make_async_copy(result.at[member, place], out_hbm.at[member, place], out_sem.at[chunk])

    for member in range(members):
        transform(member)
        filtered(member)
        inverse(member)

    def last(chunk, carry):
        finish(chunk)
        return carry

    lax.fori_loop(0, chunks, last, 0)

    def close(chunk, carry):
        saved(chunk).wait()
        each(lambda d: outward(chunk, d).wait_send())
        each(lambda d: homeward(chunk, d).wait_send())
        return carry

    lax.fori_loop(0, chunks, close, 0)
    for member in range(members):

        @pl.when(has_high)
        def _():
            halo_up(member).wait_send()

        @pl.when(has_low)
        def _():
            halo_down(member).wait_send()


def body(groups, lats, field, spectral_filter, w_in, w_out, fwd_high, fwd_low, inv_high, inv_low):
    members, rows_lat, lon_local, channels = field.shape
    hidden_units = w_in.shape[1]
    length = lon_local * groups
    modes = length // 2
    width = channels // groups
    per_member = rows_lat // HALO
    chunks = members * per_member
    columns = per_member * LANES
    filt = jnp.transpose(spectral_filter, (0, 1, 3, 2))
    dma = pltpu.SemaphoreType.DMA
    return pl.pallas_call(
        functools.partial(kernel, groups, lats),
        out_shape=jax.ShapeDtypeStruct(field.shape, F32),
        in_specs=[pl.BlockSpec(memory_space=pl.ANY)] * 8,
        out_specs=pl.BlockSpec(memory_space=pl.ANY),
        scratch_shapes=[
            pltpu.VMEM(field.shape, F32),
            pltpu.VMEM((2, TAPS, width, modes), F32),
            pltpu.VMEM((length, length), BF16),
            pltpu.VMEM((length, length), BF16),
            pltpu.VMEM((length, length), BF16),
            pltpu.VMEM((length, length), BF16),
            pltpu.VMEM(w_in.shape, BF16),
            pltpu.VMEM(w_out.shape, BF16),
            pltpu.VMEM((chunks, groups, lon_local, LANES), F32),
            pltpu.VMEM((chunks, length, LANES), F32),
            pltpu.VMEM((length, columns), BF16),
            pltpu.VMEM((length, columns), BF16),
            pltpu.VMEM((members, per_member + 2, length, LANES), F32),
            pltpu.VMEM((LANES, modes), F32),
            pltpu.VMEM((2, TAPS, modes, LANES), F32),
            pltpu.VMEM((length, columns), BF16),
            pltpu.VMEM((length, columns), BF16),
            pltpu.VMEM((chunks, length, LANES), F32),
            pltpu.VMEM((chunks, groups, lon_local, LANES), F32),
            pltpu.VMEM((HALO * lon_local, channels), F32),
            pltpu.VMEM((HALO * lon_local, channels), BF16),
            pltpu.VMEM((HALO * lon_local, hidden_units), BF16),
            pltpu.VMEM(field.shape, F32),
            dma((8,)),
            dma((chunks, groups)),
            dma((chunks, groups)),
            dma((members, 2)),
            dma((members, 2)),
            dma((chunks, groups)),
            dma((chunks, groups)),
            dma((chunks,)),
        ],
        compiler_params=pltpu.CompilerParams(
            collective_id=0, has_side_effects=True, vmem_limit_bytes=60 * 2**20
        ),
    )(field, filt, fwd_high, fwd_low, inv_high, inv_low, w_in, w_out)


def solution(mesh):
    groups, lats = mesh.shape["lon"], mesh.shape["lat"]
    in_specs = (P(None, "lat", "lon", None), P(None, None, None, "lon"), P(), P(), P(), P(), P(), P())
    out_specs = P(None, "lat", "lon", None)
    mapped = jax.shard_map(
        functools.partial(body, groups, lats), mesh=mesh, in_specs=in_specs, out_specs=out_specs, check_vma=False
    )

    def run(field, spectral_filter, w_in, w_out):
        return mapped(field, spectral_filter, w_in, w_out, *tables(field.shape[2]))

    return run
```
